512 devices in a mesh: req: 32 (over z, x), tp: 16 (over y, core).
Axes of the slice: x: 4, y: 8, z: 8, core: 2. Of those that a mesh axis runs over, the one named last changes fastest.
Arguments:
- passage_cache: bfloat16 [256, 512, 2048], P('req', None, 'tp'), may hold values from -6 to 6
- kv_weight: bfloat16 [8192, 2048], P(None, 'tp'), may hold values from -0.0625 to 0.0625
- block_hidden: bfloat16 [32, 256, 8192], P('req', None, 'tp'), may hold values from -6 to 6
- new_hidden: bfloat16 [32, 512, 8192], P('req', None, 'tp'), may hold values from -6 to 6
- queries: bfloat16 [32, 512, 8192], P('req', None, 'tp'), may hold values from -100 to 100
- passage_ids: int32 [32, 8], replicated, may hold values from 0 to 255, as said below
- passage_starts: int32 [32, 9], P('req'), may hold values from 0 to 4855, as said below
- recompute_blocks: int32 [32, 2], P('req'), may hold values from 0 to 31, as said below
- passage_counts: int32 [32], P('req'), may hold values from 1 to 8
Outputs:
- attended: bfloat16 [32, 512, 8192], P('req', None, 'tp')
The draws below stay inside these ranges and needn't reach their ends.
Inputs may be any that keep to these rules, and one draw needn't show every extreme that they name: `passage_ids`: A request's 8 entries are distinct; row i is stored on req index i // 8; no request takes more than 1 row from one req index. `passage_starts`: each row rises; its first entry is at most 255, and consecutive entries lie 512 to 575 apart. `recompute_blocks`: distinct within a request.
All inputs are finite; a program needn't handle non-finite values.
Results may differ from the reference program's by a relative error of at most 0.024.
Values may be sent and summed in bfloat16 or wider, within the bound.
No kernel may reach another device: no remote copies, remote signals or barrier semaphores. Data moves between devices by JAX's collectives and lax.ppermute only.
A program may use at most 128 MiB of HBM per device.

```python
import jax
import jax.numpy as jnp
from jax import lax

D = 8192
HQ = 64
KVH = 8
HD = 128
L = 512
BLK = 128
P_SIZE = 8
RB = 2
STORE_DEV = 8
NEW = 512
REQUESTS = 32
STORE = 256
N_REQ = 32


def draw_queries(key, part):
    key = jax.random.fold_in(key, 5)
    shape = (REQUESTS, NEW, HQ * HD)
    result = jax.random.normal(key, shape, jnp.float32)
    return jnp.clip(result, -100.0, 100.0).astype(jnp.bfloat16)


def draw_passage_ids(key, part):
    key = jax.random.fold_in(key, 1)
    capacity = (P_SIZE + N_REQ - 1) // N_REQ

    def one_row(row_key):
        first_key, second_key = jax.random.split(row_key)
        order = jax.random.permutation(first_key, N_REQ * capacity)[:P_SIZE]
        owner = order // capacity
        within = order % capacity
        base = jax.random.randint(second_key, (N_REQ,), 0, STORE_DEV)
        local = (base[owner] + within) % STORE_DEV
        return (owner * STORE_DEV + local).astype(jnp.int32)
    return jax.vmap(one_row)(jax.random.split(key, REQUESTS))


def draw_passage_starts(key, part):
    key = jax.random.fold_in(key, 2)
    gaps = jax.random.randint(key, (REQUESTS, P_SIZE + 1), 0, 64)
    lead = jax.random.randint(jax.random.fold_in(key, 1), (REQUESTS, 1), 0, 256)
    chosen = jax.random.randint(jax.random.fold_in(key, 4), (), 0, REQUESTS)
    rows = jnp.arange(REQUESTS, dtype=jnp.int32)[:, None]
    widest = rows == chosen
    lowest = rows == (chosen + 1) % REQUESTS
    gaps = jnp.where(widest, 63, gaps)
    lead = jnp.where(widest, 255, jnp.where(lowest, 0, lead))
    strides = jnp.concatenate([lead, L + gaps[:, 1:]], axis=1)
    return jnp.cumsum(strides, axis=1).astype(jnp.int32)


def draw_recompute_blocks(key, part):
    key = jax.random.fold_in(key, 3)

    def one_row(row_key):
        return jax.random.permutation(row_key, P_SIZE * L // BLK)[:RB].astype(jnp.int32)
    return jax.vmap(one_row)(jax.random.split(key, REQUESTS))


def place_ends(array, stream_key, least, top_value):
    longest = array.shape.index(max(array.shape))
    spots = []
    for shift in (0, 1):
        where = [jax.random.randint(jax.random.fold_in(stream_key, axis), (), 0, length) for axis, length in enumerate(array.shape)]
        where[longest] = (where[longest] + shift) % array.shape[longest]
        spots.append(tuple(where))
    return array.at[spots[0]].set(least).at[spots[1]].set(top_value)


def shard_levels(own_key, dims, shards, least, top_value):
    def one(axis_at, shards_of):
        steps = jax.random.uniform(jax.random.fold_in(jax.random.fold_in(own_key, 6), axis_at), (shards_of,), jnp.float32, least / len(shards), top_value / len(shards))
        return jnp.repeat(jnp.exp(steps), dims[axis_at] // shards_of).reshape((-1,) + (1,) * (len(dims) - axis_at - 1))

    gain = one(*shards[0])
    for cut in shards[1:]:
        gain = gain * one(*cut)
    return gain


def noise(rng, extent, spread, reach, shards=(), held_as=jnp.bfloat16):
    entries = jax.random.normal(rng, extent, jnp.float32) * spread
    if len(shards) > 0:
        entries = shard_levels(rng, extent, shards, -0.22, 0.18) * entries
    return jnp.clip(entries, min=-reach, max=reach).astype(held_as)


def setup_inputs(seed: int = 0) -> dict:
    streams_of = jax.random.split(jax.random.key(seed), 10)
    return {
        "passage_cache": noise(streams_of[0], (STORE, L, 2 * KVH * HD), 1.0, 6.0, ((0, 32), (2, 16))),
        "kv_weight": noise(streams_of[1], (D, 2 * KVH * HD), D ** -0.5, 0.0625, ((1, 16),)),
        "block_hidden": noise(streams_of[2], (REQUESTS, RB * BLK, D), 1.0, 6.0, ((0, 32), (2, 16))),
        "new_hidden": noise(streams_of[3], (REQUESTS, NEW, D), 1.0, 6.0, ((0, 32), (2, 16))),
        "queries": draw_queries(jax.random.fold_in(streams_of[9], 71), 0),
        "passage_ids": draw_passage_ids(jax.random.fold_in(streams_of[9], 71), 0),
        "passage_starts": draw_passage_starts(jax.random.fold_in(streams_of[9], 71), 0),
        "recompute_blocks": draw_recompute_blocks(jax.random.fold_in(streams_of[9], 71), 0),
        "passage_counts": place_ends(jax.random.randint(streams_of[8], (REQUESTS,), 1, P_SIZE + 1), jax.random.fold_in(streams_of[8], 1), 1, P_SIZE).astype(jnp.int32),
    }


THETA = 500000.0


def rotate(values, positions):
    half = HD // 2
    rates = THETA ** (-(jnp.arange(half, dtype=jnp.float32) * 2.0 / HD))
    angle = positions[:, None] * rates[None, :]
    cosine = jnp.cos(angle)[:, None, :]
    sine_part = jnp.sin(angle)[:, None, :]
    per_head = values.reshape(values.shape[0], -1, HD)
    first = per_head[:, :, :half]
    second = per_head[:, :, half:]
    turned = jnp.concatenate([first * cosine - second * sine_part, second * cosine + first * sine_part], axis=2)
    return turned.reshape(values.shape[0], -1)


def attend(query_part, key_part, value_part, allowed):
    scores = jnp.dot(query_part, key_part.T, preferred_element_type=jnp.float32) * (HD ** -0.5)
    scores = jnp.where(allowed, scores, -1e30)
    top_score = jnp.max(scores, axis=1, keepdims=True)
    weights = jnp.exp(scores - top_score)
    weights = (weights / jnp.sum(weights, axis=1, keepdims=True)).astype(jnp.bfloat16)
    return jnp.dot(weights, value_part, preferred_element_type=jnp.float32).astype(jnp.bfloat16)


def reference(passage_cache, kv_weight, block_hidden, new_hidden, queries, passage_ids, passage_starts, recompute_blocks, passage_counts):
    width = KVH * HD
    context_len = P_SIZE * L
    group_half = HQ // (2 * KVH)

    def one_request(index):
        chosen = passage_ids[index]
        starts = passage_starts[index]
        fetched = jnp.take(passage_cache, chosen, axis=0).reshape(context_len, 2 * width)
        passage_of = jnp.arange(context_len, dtype=jnp.int32) // L
        shifts = starts[passage_of].astype(jnp.float32)
        context_keys = rotate(fetched[:, :width].astype(jnp.float32), shifts).astype(jnp.bfloat16)
        context_values = fetched[:, width:]
        stacked = jnp.concatenate([block_hidden[index], new_hidden[index]], axis=0)
        projected = jnp.dot(stacked, kv_weight, preferred_element_type=jnp.float32)
        blocks = recompute_blocks[index]
        within = jnp.arange(RB * BLK, dtype=jnp.int32)
        context_index = (blocks[within // BLK] * BLK + within % BLK).astype(jnp.int32)
        block_positions = starts[context_index // L] + context_index % L
        new_positions = starts[P_SIZE] + jnp.arange(NEW, dtype=jnp.int32)
        positions = jnp.concatenate([block_positions, new_positions]).astype(jnp.float32)
        fresh_keys = rotate(projected[:, :width], positions).astype(jnp.bfloat16)
        fresh_values = projected[:, width:].astype(jnp.bfloat16)
        all_keys = context_keys.at[context_index].set(fresh_keys[:RB * BLK])
        all_values = context_values.at[context_index].set(fresh_values[:RB * BLK])
        all_keys = jnp.concatenate([all_keys, fresh_keys[RB * BLK:]], axis=0)
        all_values = jnp.concatenate([all_values, fresh_values[RB * BLK:]], axis=0)
        columns = jnp.arange(context_len + NEW, dtype=jnp.int32)
        rows_new = jnp.arange(NEW, dtype=jnp.int32)
        in_context = columns < context_len
        allowed = jnp.where(in_context[None, :], (columns // L)[None, :] < passage_counts[index], (columns - context_len)[None, :] <= rows_new[:, None])
        query_rows = queries[index]

        def one_head(head):
            kv_head = (head % (HQ // 2)) // group_half
            query_part = lax.dynamic_slice_in_dim(query_rows, head * HD, HD, 1)
            key_part = lax.dynamic_slice_in_dim(all_keys, kv_head * HD, HD, 1)
            value_part = lax.dynamic_slice_in_dim(all_values, kv_head * HD, HD, 1)
            return attend(query_part, key_part, value_part, allowed)

        outputs = lax.map(one_head, jnp.arange(HQ, dtype=jnp.int32))
        return jnp.transpose(outputs, (1, 0, 2)).reshape(NEW, HQ * HD)

    return lax.map(one_request, jnp.arange(REQUESTS, dtype=jnp.int32))
```

```python
import functools

import jax
import jax.numpy as jnp
from jax import lax
from jax.experimental import pallas as pl
from jax.experimental.pallas import tpu as pltpu
from jax.sharding import PartitionSpec as P

HD = 128
THETA = 500000.0
LOG2E = 1.4426950408889634
SCALE = HD ** (-0.5) * LOG2E
NEG = -1e30
QT = 256
KC = 512
BLK = 128
F32 = jnp.float32
BF16 = jnp.bfloat16
GROUPS = ((0, 4), (4, 8))


def tables(positions):
    rates = THETA ** (-(jnp.arange(HD // 2, dtype=F32) * 2.0 / HD))
    angle = positions.astype(F32)[:, None] * rates[None, :]
    cosine, sine = jnp.cos(angle), jnp.sin(angle)
    return jnp.concatenate([cosine, cosine], axis=1), jnp.concatenate([-sine, sine], axis=1)


def turn(values, cosine, sine):
    half = HD // 2
    swapped = jnp.concatenate([values[:, half:], values[:, :half]], axis=1)
    return values * cosine + swapped * sine


def partner(block, tp_total):
    half = tp_total // 2
    return lax.ppermute(block, "tp", [(i, (i + half) % tp_total) for i in range(tp_total)])


def pick_kernel(count, ids, pieces, out):
    def step(i, _):
        out[i] = pieces[ids[i]]
        return 0

    lax.fori_loop(0, count, step, 0, unroll=16)


def pick(pieces, ids):
    count = ids.shape[0]
    return pl.pallas_call(
        functools.partial(pick_kernel, count),
        out_shape=jax.ShapeDtypeStruct((count,) + pieces.shape[1:], pieces.dtype),
        in_specs=[pl.BlockSpec(memory_space=pltpu.SMEM), pl.BlockSpec(memory_space=pltpu.VMEM)],
        out_specs=pl.BlockSpec(memory_space=pltpu.VMEM),
        compiler_params=pltpu.CompilerParams(vmem_limit_bytes=16 * 2**20),
        cost_estimate=pl.CostEstimate(flops=0, bytes_accessed=count * 8192, transcendentals=0),
        name="pick",
    )(ids, pieces)


def scores_into(store, keys, kx, weights, causal_from, column):
    top = None
    for c in range(0, keys, BLK * 2):
        part = jnp.dot(kx[c : c + BLK * 2, :], weights, preferred_element_type=F32)
        if causal_from is not None and c >= causal_from:
            row = lax.broadcasted_iota(jnp.int32, part.shape, 0) + (c - causal_from)
            query = lax.broadcasted_iota(jnp.int32, part.shape, 1) + column
            part = jnp.where(row <= query, part, NEG)
        store[c : c + BLK * 2, :] = part
        high = jnp.max(part.reshape(BLK * 2 // 8, 8, part.shape[1]), axis=0)
        top = high if top is None else jnp.maximum(top, high)
    return jnp.max(top, axis=0, keepdims=True) * SCALE


def weigh(store, keys, vt, top):
    total = None
    for c in range(0, keys, BLK * 2):
        weights = jnp.exp2(store[c : c + BLK * 2, :] * SCALE - top).astype(BF16)
        part = jnp.dot(vt[:, c : c + BLK * 2], weights, preferred_element_type=F32)
        total = part if total is None else total + part
    return total


def fill_queries(q_ref, qx, heads, rows):
    for h in range(heads):
        qx[0:HD, h * rows : (h + 1) * rows] = q_ref[:, h * HD : (h + 1) * HD].T
    first = lax.broadcasted_iota(jnp.int32, (HD, heads * rows), 0) == 0
    qx[HD:, :] = jnp.where(first, 1.0, 0.0).astype(BF16)


def bias_block(value):
    lane = lax.broadcasted_iota(jnp.int32, (BLK, HD), 1)
    return jnp.where(lane == 0, value, 0.0).astype(BF16)


def run_tiles(tiles, keys, kx, vt, qx, sa, sb, rows, causal_from, put):
    def weights_of(i):
        return qx[:, pl.ds(pl.multiple_of(i * QT, QT), QT)]

    def column_of(i):
        return lax.rem(i * QT, rows)

    top = scores_into(sa, keys, kx, weights_of(0), causal_from, 0)

    def step(j, top_a):
        i = 2 * j
        top_b = scores_into(sb, keys, kx, weights_of(i + 1), causal_from, column_of(i + 1))
        put(i, top_a, weigh(sa, keys, vt, top_a))
        later = jnp.minimum(i + 2, tiles - 1)
        top_a = scores_into(sa, keys, kx, weights_of(later), causal_from, column_of(later))
        put(i + 1, top_b, weigh(sb, keys, vt, top_b))
        return top_a

    lax.fori_loop(0, tiles // 2, step, top)


def context_kernel(low, high, sizes, scalars, q_ref, cos_ref, sin_ref, own, other, total, tops, qx, kx, vt, sa, sb):
    heads, rows, length = sizes
    keys = (high - low) * length
    is_key = scalars[0] == 1
    fill_queries(q_ref, qx, heads, rows)
    vt[HD:, :] = jnp.ones((16, keys), BF16)
    for s in range(high - low):
        mine = own[:, s].reshape(length, HD)
        theirs = other[:, s].reshape(length, HD)
        raw = jnp.where(is_key, mine, theirs).astype(F32)
        cosine = cos_ref[low + s : low + s + 1, :]
        sine = sin_ref[low + s : low + s + 1, :]
        base = s * length
        kx[base : base + length, :HD] = (raw * cosine + pltpu.roll(raw, HD // 2, 1) * sine).astype(BF16)
        vt[:HD, base : base + length] = jnp.where(is_key, theirs, mine).T
        for b in range(length // BLK):
            number = (low + s) * (length // BLK) + b
            hidden = jnp.logical_or(number == scalars[2], number == scalars[3])
            hidden = jnp.logical_or(hidden, low + s >= scalars[1])
            kx[base + b * BLK : base + (b + 1) * BLK, HD:] = bias_block(jnp.where(hidden, NEG, 0.0))

    def put(i, top, part):
        at = pl.ds(pl.multiple_of(i * QT, QT), QT)
        total[:, at] = part
        tops[:, at] = jnp.broadcast_to(top, (8, QT))

    run_tiles(heads * rows // QT, keys, kx, vt, qx, sa, sb, rows, None, put)


def fresh_kernel(sizes, parts, scalars, q_ref, own, other, *rest):
    heads, rows, length = sizes
    states = rest[: 2 * parts]
    out, qx, kx, vt, sa, sb = rest[2 * parts :]
    keys = own.shape[0]
    block_rows = keys - rows
    is_key = scalars[0] == 1
    fill_queries(q_ref, qx, heads, rows)
    vt[HD:, :] = jnp.ones((16, keys), BF16)
    kx[:, :HD] = jnp.where(is_key, own[...], other[...])
    vt[:HD, :] = jnp.where(is_key, other[...], own[...]).T
    for b in range(keys // BLK):
        value = 0.0
        if b * BLK < block_rows:
            value = jnp.where(scalars[2 + b] // (length // BLK) >= scalars[1], NEG, 0.0)
        kx[b * BLK : (b + 1) * BLK, HD:] = bias_block(value)

    def put(i, top, part):
        at = pl.ds(pl.multiple_of(i * QT, QT), QT)
        tops = [states[2 * n + 1][0:1, at] for n in range(parts)]
        best = functools.reduce(jnp.maximum, tops, top)
        joined = part * jnp.exp2(top - best)
        for n in range(parts):
            joined = joined + states[2 * n][:, at] * jnp.exp2(tops[n] - best)
        result = joined[:HD] / joined[HD : HD + 1]
        row = lax.rem(i * QT, rows)
        head = lax.div(i * QT, rows)
        out[
            pl.ds(pl.multiple_of(row, QT), QT), pl.ds(pl.multiple_of(head * HD, HD), HD)
        ] = result.T.astype(BF16)

    run_tiles(heads * rows // QT, keys, kx, vt, qx, sa, sb, rows, block_rows, put)


VMEM = pl.BlockSpec(memory_space=pltpu.VMEM)
SMEM = pl.BlockSpec(memory_space=pltpu.SMEM)


def scratch(keys, columns):
    return [
        pltpu.VMEM((2 * HD, columns), BF16),
        pltpu.VMEM((keys, 2 * HD), BF16),
        pltpu.VMEM((HD + 16, keys), BF16),
        pltpu.VMEM((keys, QT), F32),
        pltpu.VMEM((keys, QT), F32),
    ]


def cost(keys, columns):
    return pl.CostEstimate(
        flops=4 * keys * columns * HD, bytes_accessed=4 * keys * HD * 2, transcendentals=keys * columns
    )


def context_part(low, high, sizes, scalars, query_rows, cosine, sine, own, other):
    heads, rows, length = sizes
    keys, columns = (high - low) * length, heads * rows
    return pl.pallas_call(
        functools.partial(context_kernel, low, high, sizes),
        out_shape=(
            jax.ShapeDtypeStruct((HD + 16, columns), F32),
            jax.ShapeDtypeStruct((8, columns), F32),
        ),
        in_specs=[SMEM] + [VMEM] * 5,
        out_specs=(VMEM, VMEM),
        scratch_shapes=scratch(keys, columns),
        compiler_params=pltpu.CompilerParams(vmem_limit_bytes=32 * 2**20),
        cost_estimate=cost(keys, columns),
        name="context_part",
    )(scalars, query_rows, cosine, sine, own, other)


def fresh_part(sizes, scalars, query_rows, own, other, states):
    heads, rows, length = sizes
    keys, columns = own.shape[0], heads * rows
    flat = [array for state in states for array in state]
    return pl.pallas_call(
        functools.partial(fresh_kernel, sizes, len(states)),
        out_shape=jax.ShapeDtypeStruct((rows, heads * HD), BF16),
        in_specs=[SMEM] + [VMEM] * (3 + len(flat)),
        out_specs=VMEM,
        scratch_shapes=scratch(keys, columns),
        compiler_params=pltpu.CompilerParams(vmem_limit_bytes=32 * 2**20),
        cost_estimate=cost(keys, columns),
        name="fresh_part",
    )(scalars, query_rows, own, other, *flat)


def body(
    passage_cache,
    kv_weight,
    block_hidden,
    new_hidden,
    queries,
    passage_ids,
    passage_starts,
    recompute_blocks,
    passage_counts,
):
    req_total = lax.axis_size("req")
    tp_total = lax.axis_size("tp")
    tp_index = lax.axis_index("tp")
    store_dev, length, local_cols = passage_cache.shape
    passages = passage_ids.shape[1]
    piece = length // req_total
    starts = passage_starts[0]
    blocks = recompute_blocks[0]
    is_key = tp_index < tp_total // 2
    scalars = jnp.concatenate(
        [is_key.astype(jnp.int32)[None], passage_counts.astype(jnp.int32), blocks.astype(jnp.int32)]
    )

    outgoing = passage_cache.reshape(store_dev, req_total, piece, local_cols).transpose(1, 0, 2, 3)
    pieces = lax.all_to_all(outgoing, "req", split_axis=0, concat_axis=0, tiled=True)
    pieces = pieces.reshape(req_total * store_dev, piece, local_cols)

    fetched = []
    for low, high in GROUPS:
        ids = passage_ids[:, low:high].reshape(-1)
        send = pick(pieces, ids).reshape(req_total, high - low, piece, local_cols)
        fetched.append(lax.all_to_all(send, "req", split_axis=0, concat_axis=0, tiled=True))
    crossed = [partner(rows, tp_total) for rows in fetched]

    block_rows = block_hidden.shape[1]
    new_count = new_hidden.shape[1]
    local_stack = jnp.concatenate([block_hidden[0], new_hidden[0]], axis=0)
    projected = jnp.dot(
        lax.all_gather(local_stack, "tp", axis=1, tiled=True), kv_weight, preferred_element_type=F32
    )
    block_size = block_rows // blocks.shape[0]
    within = jnp.arange(block_rows, dtype=jnp.int32)
    context_index = blocks[within // block_size] * block_size + within % block_size
    block_positions = starts[context_index // length] + context_index % length
    new_positions = starts[passages] + jnp.arange(new_count, dtype=jnp.int32)
    turned = turn(projected, *tables(jnp.concatenate([block_positions, new_positions])))
    fresh = jnp.where(is_key, turned, projected).astype(BF16)
    fresh_other = partner(fresh, tp_total)

    query_rows = queries[0]
    sizes = (query_rows.shape[1] // HD, new_count, length)
    cosine, sine = tables(starts[:passages])
    states = [
        context_part(low, high, sizes, scalars, query_rows, cosine, sine, own, other)
        for (low, high), own, other in zip(GROUPS, fetched, crossed)
    ]
    return fresh_part(sizes, scalars, query_rows, fresh, fresh_other, states)[None]


def solution(mesh):
    in_specs = (
        P("req", None, "tp"),
        P(None, "tp"),
        P("req", None, "tp"),
        P("req", None, "tp"),
        P("req", None, "tp"),
        P(),
        P("req", None),
        P("req", None),
        P("req"),
    )
    out_specs = P("req", None, "tp")
    return jax.shard_map(body, mesh=mesh, in_specs=in_specs, out_specs=out_specs, check_vma=False)
```

```python
import functools

import jax
import jax.numpy as jnp
from jax import lax
from jax.experimental import pallas as pl
from jax.experimental.pallas import tpu as pltpu
from jax.sharding import PartitionSpec as P

HD = 128
THETA = 500000.0
LOG2E = 1.4426950408889634
SCALE = HD ** (-0.5) * LOG2E
NEG = -1e30
QT = 256
KC = 512
BLK = 128
F32 = jnp.float32
BF16 = jnp.bfloat16
GROUPS = ((0, 4), (4, 8))


def tables(positions):
    rates = THETA ** (-(jnp.arange(HD // 2, dtype=F32) * 2.0 / HD))
    angle = positions.astype(F32)[:, None] * rates[None, :]
    cosine, sine = jnp.cos(angle), jnp.sin(angle)
    return jnp.concatenate([cosine, cosine], axis=1), jnp.concatenate([-sine, sine], axis=1)


def turn(values, cosine, sine):
    half = HD // 2
    swapped = jnp.concatenate([values[:, half:], values[:, :half]], axis=1)
    return values * cosine + swapped * sine


def partner(block, tp_total):
    half = tp_total // 2
    return lax.ppermute(block, "tp", [(i, (i + half) % tp_total) for i in range(tp_total)])


def pick_kernel(count, ids, pieces, out):
    def step(i, _):
        out[i] = pieces[ids[i]]
        return 0

    lax.fori_loop(0, count, step, 0, unroll=16)


def pick(pieces, ids):
    count = ids.shape[0]
    return pl.pallas_call(
        functools.partial(pick_kernel, count),
        out_shape=jax.ShapeDtypeStruct((count,) + pieces.shape[1:], pieces.dtype),
        in_specs=[pl.BlockSpec(memory_space=pltpu.SMEM), pl.BlockSpec(memory_space=pltpu.VMEM)],
        out_specs=pl.BlockSpec(memory_space=pltpu.VMEM),
        compiler_params=pltpu.CompilerParams(vmem_limit_bytes=16 * 2**20),
        cost_estimate=pl.CostEstimate(flops=0, bytes_accessed=count * 8192, transcendentals=0),
        name="pick",
    )(ids, pieces)


def scores_into(store, keys, kx, weights, causal_from, column):
    top = None
    for c in range(0, keys, BLK * 2):
        part = jnp.dot(kx[c : c + BLK * 2, :], weights, preferred_element_type=F32)
        if causal_from is not None and c >= causal_from:
            row = lax.broadcasted_iota(jnp.int32, part.shape, 0) + (c - causal_from)
            query = lax.broadcasted_iota(jnp.int32, part.shape, 1) + column
            part = jnp.where(row <= query, part, NEG)
        store[c : c + BLK * 2, :] = part
        high = jnp.max(part.reshape(BLK * 2 // 8, 8, part.shape[1]), axis=0)
        top = high if top is None else jnp.maximum(top, high)
    return jnp.max(top, axis=0, keepdims=True) * SCALE


def weigh(store, keys, vt, top):
    total = None
    for c in range(0, keys, BLK * 2):
        weights = jnp.exp2(store[c : c + BLK * 2, :] * SCALE - top).astype(BF16)
        part = jnp.dot(vt[:, c : c + BLK * 2], weights, preferred_element_type=F32)
        total = part if total is None else total + part
    return total


def fill_queries(q_ref, qx, heads, rows):
    for h in range(heads):
        qx[0:HD, h * rows : (h + 1) * rows] = q_ref[:, h * HD : (h + 1) * HD].T
    first = lax.broadcasted_iota(jnp.int32, (HD, heads * rows), 0) == 0
    qx[HD:, :] = jnp.where(first, 1.0, 0.0).astype(BF16)


def bias_block(value):
    lane = lax.broadcasted_iota(jnp.int32, (BLK, HD), 1)
    return jnp.where(lane == 0, value, 0.0).astype(BF16)


def run_tiles(tiles, keys, kx, vt, qx, sa, sb, rows, causal_from, put):
    def weights_of(i):
        return qx[:, pl.ds(pl.multiple_of(i * QT, QT), QT)]

    def column_of(i):
        return lax.rem(i * QT, rows)

    top = scores_into(sa, keys, kx, weights_of(0), causal_from, 0)

    def step(j, top_a):
        i = 2 * j
        top_b = scores_into(sb, keys, kx, weights_of(i + 1), causal_from, column_of(i + 1))
        put(i, top_a, weigh(sa, keys, vt, top_a))
        later = jnp.minimum(i + 2, tiles - 1)
        top_a = scores_into(sa, keys, kx, weights_of(later), causal_from, column_of(later))
        put(i + 1, top_b, weigh(sb, keys, vt, top_b))
        return top_a

    lax.fori_loop(0, tiles // 2, step, top)


def context_kernel(low, high, sizes, scalars, q_ref, cos_ref, sin_ref, own, other, *rest):
    total, tops, qx, kx, vt, sa, sb = rest[-7:]
    heads, rows, length = sizes
    keys = (high - low) * length
    is_key = scalars[0] == 1
    fill_queries(q_ref, qx, heads, rows)
    vt[HD:, :] = jnp.ones((16, keys), BF16)
    for s in range(high - low):
        mine = own[:, s].reshape(length, HD)
        theirs = other[:, s].reshape(length, HD)
        raw = jnp.where(is_key, mine, theirs).astype(F32)
        cosine = cos_ref[low + s : low + s + 1, :]
        sine = sin_ref[low + s : low + s + 1, :]
        base = s * length
        kx[base : base + length, :HD] = (raw * cosine + pltpu.roll(raw, HD // 2, 1) * sine).astype(BF16)
        vt[:HD, base : base + length] = jnp.where(is_key, theirs, mine).T
        for b in range(length // BLK):
            number = (low + s) * (length // BLK) + b
            hidden = jnp.logical_or(number == scalars[2], number == scalars[3])
            hidden = jnp.logical_or(hidden, low + s >= scalars[1])
            kx[base + b * BLK : base + (b + 1) * BLK, HD:] = bias_block(jnp.where(hidden, NEG, 0.0))

    def put(i, top, part):
        at = pl.ds(pl.multiple_of(i * QT, QT), QT)
        total[:, at] = part
        tops[:, at] = jnp.broadcast_to(top, (8, QT))

    run_tiles(heads * rows // QT, keys, kx, vt, qx, sa, sb, rows, None, put)


def fresh_kernel(sizes, parts, scalars, q_ref, own, other, *rest):
    heads, rows, length = sizes
    states = rest[: 2 * parts]
    out, qx, kx, vt, sa, sb = rest[2 * parts :]
    keys = own.shape[0]
    block_rows = keys - rows
    is_key = scalars[0] == 1
    fill_queries(q_ref, qx, heads, rows)
    vt[HD:, :] = jnp.ones((16, keys), BF16)
    kx[:, :HD] = jnp.where(is_key, own[...], other[...])
    vt[:HD, :] = jnp.where(is_key, other[...], own[...]).T
    for b in range(keys // BLK):
        value = 0.0
        if b * BLK < block_rows:
            value = jnp.where(scalars[2 + b] // (length // BLK) >= scalars[1], NEG, 0.0)
        kx[b * BLK : (b + 1) * BLK, HD:] = bias_block(value)

    def put(i, top, part):
        at = pl.ds(pl.multiple_of(i * QT, QT), QT)
        tops = [states[2 * n + 1][0:1, at] for n in range(parts)]
        best = functools.reduce(jnp.maximum, tops, top)
        joined = part * jnp.exp2(top - best)
        for n in range(parts):
            joined = joined + states[2 * n][:, at] * jnp.exp2(tops[n] - best)
        result = joined[:HD] / joined[HD : HD + 1]
        row = lax.rem(i * QT, rows)
        head = lax.div(i * QT, rows)
        out[
            pl.ds(pl.multiple_of(row, QT), QT), pl.ds(pl.multiple_of(head * HD, HD), HD)
        ] = result.T.astype(BF16)

    run_tiles(heads * rows // QT, keys, kx, vt, qx, sa, sb, rows, block_rows, put)


VMEM = pl.BlockSpec(memory_space=pltpu.VMEM)
SMEM = pl.BlockSpec(memory_space=pltpu.SMEM)


def scratch(keys, columns):
    return [
        pltpu.VMEM((2 * HD, columns), BF16),
        pltpu.VMEM((keys, 2 * HD), BF16),
        pltpu.VMEM((HD + 16, keys), BF16),
        pltpu.VMEM((keys, QT), F32),
        pltpu.VMEM((keys, QT), F32),
    ]


def cost(keys, columns):
    return pl.CostEstimate(
        flops=4 * keys * columns * HD, bytes_accessed=4 * keys * HD * 2, transcendentals=keys * columns
    )


def context_part(low, high, sizes, scalars, query_rows, cosine, sine, own, other, after):
    heads, rows, length = sizes
    keys, columns = (high - low) * length, heads * rows
    return pl.pallas_call(
        functools.partial(context_kernel, low, high, sizes),
        out_shape=(
            jax.ShapeDtypeStruct((HD + 16, columns), F32),
            jax.ShapeDtypeStruct((8, columns), F32),
        ),
        in_specs=[SMEM] + [VMEM] * 5 + [pl.BlockSpec(memory_space=pl.ANY)] * len(after),
        out_specs=(VMEM, VMEM),
        scratch_shapes=scratch(keys, columns),
        compiler_params=pltpu.CompilerParams(vmem_limit_bytes=32 * 2**20),
        cost_estimate=cost(keys, columns),
        name="context_part",
    )(scalars, query_rows, cosine, sine, own, other, *after)


def fresh_part(sizes, scalars, query_rows, own, other, states):
    heads, rows, length = sizes
    keys, columns = own.shape[0], heads * rows
    flat = [array for state in states for array in state]
    return pl.pallas_call(
        functools.partial(fresh_kernel, sizes, len(states)),
        out_shape=jax.ShapeDtypeStruct((rows, heads * HD), BF16),
        in_specs=[SMEM] + [VMEM] * (3 + len(flat)),
        out_specs=VMEM,
        scratch_shapes=scratch(keys, columns),
        compiler_params=pltpu.CompilerParams(vmem_limit_bytes=32 * 2**20),
        cost_estimate=cost(keys, columns),
        name="fresh_part",
    )(scalars, query_rows, own, other, *flat)


def body(
    passage_cache,
    kv_weight,
    block_hidden,
    new_hidden,
    queries,
    passage_ids,
    passage_starts,
    recompute_blocks,
    passage_counts,
):
    req_total = lax.axis_size("req")
    tp_total = lax.axis_size("tp")
    tp_index = lax.axis_index("tp")
    store_dev, length, local_cols = passage_cache.shape
    passages = passage_ids.shape[1]
    piece = length // req_total
    starts = passage_starts[0]
    blocks = recompute_blocks[0]
    is_key = tp_index < tp_total // 2
    scalars = jnp.concatenate(
        [is_key.astype(jnp.int32)[None], passage_counts.astype(jnp.int32), blocks.astype(jnp.int32)]
    )

    outgoing = passage_cache.reshape(store_dev, req_total, piece, local_cols).transpose(1, 0, 2, 3)
    pieces = lax.all_to_all(outgoing, "req", split_axis=0, concat_axis=0, tiled=True)
    pieces = pieces.reshape(req_total * store_dev, piece, local_cols)

    fetched = []
    for low, high in GROUPS:
        ids = passage_ids[:, low:high].reshape(-1)
        send = pick(pieces, ids).reshape(req_total, high - low, piece, local_cols)
        fetched.append(lax.all_to_all(send, "req", split_axis=0, concat_axis=0, tiled=True))
    crossed = [partner(rows, tp_total) for rows in fetched]

    block_rows = block_hidden.shape[1]
    new_count = new_hidden.shape[1]
    local_stack = jnp.concatenate([block_hidden[0], new_hidden[0]], axis=0)
    projected = jnp.dot(
        lax.all_gather(local_stack, "tp", axis=1, tiled=True), kv_weight, preferred_element_type=F32
    )
    block_size = block_rows // blocks.shape[0]
    within = jnp.arange(block_rows, dtype=jnp.int32)
    context_index = blocks[within // block_size] * block_size + within % block_size
    block_positions = starts[context_index // length] + context_index % length
    new_positions = starts[passages] + jnp.arange(new_count, dtype=jnp.int32)
    turned = turn(projected, *tables(jnp.concatenate([block_positions, new_positions])))
    fresh = jnp.where(is_key, turned, projected).astype(BF16)
    fresh_other = partner(fresh, tp_total)

    query_rows = queries[0]
    sizes = (query_rows.shape[1] // HD, new_count, length)
    cosine, sine = tables(starts[:passages])
    states = [
        context_part(low, high, sizes, scalars, query_rows, cosine, sine, own, other, (fresh,))
        for (low, high), own, other in zip(GROUPS, fetched, crossed)
    ]
    return fresh_part(sizes, scalars, query_rows, fresh, fresh_other, states)[None]


def solution(mesh):
    in_specs = (
        P("req", None, "tp"),
        P(None, "tp"),
        P("req", None, "tp"),
        P("req", None, "tp"),
        P("req", None, "tp"),
        P(),
        P("req", None),
        P("req", None),
        P("req"),
    )
    out_specs = P("req", None, "tp")
    return jax.shard_map(body, mesh=mesh, in_specs=in_specs, out_specs=out_specs, check_vma=False)
```
